32 devices in a mesh: layer: 4 (over z), panel: 8 (over y, x, core).
Axes of the slice: x: 2, y: 2, z: 4, core: 2. Of those that a mesh axis runs over, the one named last changes fastest.
Arguments:
- reflections: float32 [32, 1024, 1024], P(None, 'panel'), may hold values from -0.95 to 0.95
- wave_decay: float32 [32, 1024], replicated, may hold values from 0.3 to 3
- thickness: float32 [4], P('layer'), may hold values from 0.4 to 1
- material: int32 [4], P('layer'), may hold values from 0 to 31
Outputs:
- stack_blocks: float32 [4, 1024, 1024], P('layer', 'panel')
The draws below stay inside these ranges and needn't reach their ends.
All inputs are finite; a program needn't handle non-finite values.
Results may differ from the reference program's by a relative error of at most 0.00014.
Values sent between devices are 32-bit elements; how exact they have to be, the bound alone decides.
A program may use at most 128 MiB of HBM per device.

```python
import math
import jax
import jax.numpy as jnp
from jax import lax

ORDER = 1024
MATERIALS = 32
TERMS = 6
LAYERS = 4


def draw_reflections(key, part):
    key_mag = jax.random.fold_in(key, 11)
    key_sign = jax.random.fold_in(key, 12)
    key_off = jax.random.fold_in(key, 13)
    shape = (MATERIALS, ORDER, ORDER)
    diag_mag = jax.random.uniform(key_mag, (MATERIALS, ORDER), jnp.float32, 0.6, 0.9)
    signs = jnp.where(jax.random.bernoulli(key_sign, 0.5, (MATERIALS, ORDER)), 1.0, -1.0)
    spread = 0.16 / math.sqrt(ORDER)
    off_part = jax.random.truncated_normal(key_off, -4.0, 4.0, shape, jnp.float32) * spread
    row_ids = lax_rows(shape)
    col_ids = lax_cols(shape)
    identity = jnp.where(row_ids == col_ids, 1.0, 0.0).astype(jnp.float32)
    return off_part * (1.0 - identity) + identity * (diag_mag * signs)[:, :, None]


def lax_rows(shape):
    return jnp.broadcast_to(jnp.arange(shape[1], dtype=jnp.int32)[None, :, None], shape)


def lax_cols(shape):
    return jnp.broadcast_to(jnp.arange(shape[2], dtype=jnp.int32)[None, None, :], shape)


def plant(values, key, smallest, top_value):
    longest = values.shape.index(max(values.shape))
    spots = []
    for shift in (0, 1):
        where = [jax.random.randint(jax.random.fold_in(key, axis), (), 0, length) for axis, length in enumerate(values.shape)]
        where[longest] = (where[longest] + shift) % values.shape[longest]
        spots.append(tuple(where))
    return values.at[spots[0]].set(smallest).at[spots[1]].set(top_value)


def level_of(own_key, shape, shards, low, top_value):
    loudness, own = 1.0, jax.random.fold_in(own_key, 6)
    for position, shards_of in shards:
        draws = jnp.exp(jax.random.uniform(jax.random.fold_in(own, position), (shards_of,), jnp.float32, low / len(shards), top_value / len(shards)))
        loudness = loudness * jnp.repeat(draws, shape[position] // shards_of).reshape([-1 if axis == position else 1 for axis in range(len(shape))])
    return loudness


def setup_inputs(seed: int = 0) -> dict:
    splits = jax.random.split(jax.random.key(seed), 5)
    return {
        "reflections": draw_reflections(jax.random.fold_in(splits[4], 71), 0),
        "wave_decay": jnp.clip(jnp.exp(jax.random.uniform(splits[1], (MATERIALS, ORDER), jnp.float32, math.log(0.3), math.log(3.0))), 0.3, 3.0),
        "thickness": jnp.clip(0.4 + 0.6 * jax.random.uniform(splits[2], (LAYERS,), jnp.float32) ** level_of(splits[2], (LAYERS,), ((0, 4),), -0.2, 0.2), 0.4, 1.0),
        "material": plant(jax.random.randint(splits[3], (LAYERS,), 0, MATERIALS), jax.random.fold_in(splits[3], 1), 0, MATERIALS - 1).astype(jnp.int32),
    }


def product(left_side, right_side):
    return jnp.dot(left_side, right_side, precision=lax.Precision.HIGHEST, preferred_element_type=jnp.float32)


def series_sum(start_rows, factor_one, factor_two):
    term_now = start_rows
    summed = start_rows
    for _ in range(TERMS - 1):
        term_now = product(product(term_now, factor_one), factor_two)
        summed = summed + term_now
    return summed


def build_layer(refl_full, decays):
    identity = jnp.eye(refl_full.shape[0], dtype=jnp.float32)
    scaled_refl = decays[:, None] * refl_full
    summed = series_sum(identity, scaled_refl, scaled_refl)
    numer = decays[:, None] * refl_full * decays[None, :] - refl_full
    reflect_block = product(summed, numer)
    scaled_sum = summed * decays[None, :]
    trans_block = scaled_sum - product(product(scaled_sum, refl_full), refl_full)
    return (reflect_block, trans_block, trans_block, reflect_block)


def star_product(front_part, back_part):
    upper_chain = series_sum(front_part[1], back_part[0], front_part[3])
    lower_chain = series_sum(back_part[2], front_part[3], back_part[0])
    block_one = front_part[0] + product(product(upper_chain, back_part[0]), front_part[2])
    block_two = product(upper_chain, back_part[1])
    block_three = product(lower_chain, front_part[2])
    block_four = back_part[3] + product(product(lower_chain, front_part[3]), back_part[1])
    return (block_one, block_two, block_three, block_four)


def reference(reflections, wave_decay, thickness, material):
    stacks = []
    for layer_index in range(LAYERS):
        chosen = material[layer_index].astype(jnp.int32)
        refl_full = lax.dynamic_index_in_dim(reflections, chosen, 0, keepdims=False)
        decays = jnp.exp(-lax.dynamic_index_in_dim(wave_decay, chosen, 0, keepdims=False) * thickness[layer_index])
        stacks.append(build_layer(refl_full, decays))
    while len(stacks) > 1:
        stacks = [star_product(stacks[2 * pair], stacks[2 * pair + 1]) for pair in range(len(stacks) // 2)]
    return jnp.stack(stacks[0])
```

```python
import jax
import jax.numpy as jnp
from jax import lax
from jax.sharding import PartitionSpec as P

TERMS = 6


def product(left_side, right_side):
    return jnp.dot(
        left_side, right_side, precision=lax.Precision.HIGH, preferred_element_type=jnp.float32
    )


def gathered(rows):
    return lax.all_gather(rows, "panel", axis=0, tiled=True)


def chain(start, one, two):
    now, summed = start, start
    for _ in range(TERMS - 1):
        now = product(product(now, one), two)
        summed = summed + now
    return summed


def local(reflections, wave_decay, thickness, material):
    rows, order = reflections.shape[1:]
    me = lax.axis_index("panel")
    layer = lax.axis_index("layer")
    chosen = material[0]
    refl_rows = lax.dynamic_index_in_dim(reflections, chosen, 0, keepdims=False)
    decays = jnp.exp(
        -lax.dynamic_index_in_dim(wave_decay, chosen, 0, keepdims=False) * thickness[0]
    )
    own_decays = lax.dynamic_slice_in_dim(decays, me * rows, rows)
    refl = gathered(refl_rows)
    now = own_decays[:, None] * refl_rows
    ids = me * rows + jnp.arange(rows, dtype=jnp.int32)
    even = jnp.where(ids[:, None] == jnp.arange(order)[None, :], 1.0, 0.0).astype(jnp.float32)
    odd = now
    for _ in range(TERMS - 1):
        now = product(now * decays, refl)
        even = even + now
        now = product(now * decays, refl)
        odd = odd + now
    both = product(jnp.concatenate([even, odd]), refl)
    r_own = odd * decays - both[:rows]
    t_own = even * decays - both[rows:]
    r_other, t_other = lax.ppermute(
        (r_own, t_own), "layer", [(0, 1), (1, 0), (2, 3), (3, 2)]
    )
    r_a, r_b, t_a = gathered(r_own), gathered(r_other), gathered(t_own)
    summed = chain(jnp.concatenate([product(t_own, r_b), t_other]), r_a, r_b)
    done = product(summed, t_a)
    out1, out2 = r_own + done[:rows], done[rows:]
    inner = (layer == 1) | (layer == 2)
    near1, near2 = lax.ppermute((out1, out2), "layer", [(1, 0), (2, 3)])
    across = lax.ppermute(out1, "layer", [(1, 2), (2, 1)])
    far = lax.ppermute(out1, "layer", [(1, 3), (2, 0)])
    last = lax.ppermute(out2, "layer", [(0, 2), (3, 1)])
    h1 = gathered(jnp.where(inner, out1, near1))
    h2 = gathered(jnp.where(inner, across, far))
    end = gathered(jnp.where(inner, last, out2))
    summed = chain(jnp.where(inner, out2, near2), h2, h1)
    summed = jnp.where(inner, summed, product(summed, h2))
    return (jnp.where(inner, 0.0, out1) + product(summed, end))[None]


def solution(mesh):
    placed = (P(None, "panel", None), P(), P("layer"), P("layer"))
    return jax.shard_map(
        local, mesh=mesh, in_specs=placed, out_specs=P("layer", "panel", None), check_vma=False
    )
```

```python
import functools

import jax
import jax.numpy as jnp
from jax import lax
from jax.experimental import pallas as pl
from jax.experimental.pallas import tpu as pltpu
from jax.sharding import PartitionSpec as P

TERMS = 6
TILE = 256
MESH = pl.DeviceIdType.MESH


def kernel(
    n, rows, order,
    refl_ref, decay_ref, own_decay_ref, out_ref,
    land_f, land_ra, land_rb, land_ta, land_h1, land_h2, land_l,
    whi, wlo, lhs, now, mid, acc, t_other, start1, out1, out2,
    send_sem, recv_sem, zsend, zrecv,
):
    layer = lax.axis_index("layer")
    me = lax.axis_index("panel")
    half = rows // 2
    core_bit = 1
    chip_bits = [1 << i for i in range(1, n.bit_length() - 1)]
    inner = (layer == 1) | (layer == 2)
    outer = (layer == 0) | (layer == 3)

    def moved(mask):
        place = me
        bit = 1
        while bit < n:
            if mask & bit:
                place = place + bit * (1 - 2 * (me // bit % 2))
            bit *= 2
        return place

    barrier = pltpu.get_barrier_semaphore()
    for bit in chip_bits + [core_bit]:
        pl.semaphore_signal(barrier, inc=1, device_id=(layer, moved(bit)), device_id_type=MESH)
    for step in range(1, 4):
        pl.semaphore_signal(
            barrier, inc=1, device_id=((layer + step) % 4, me), device_id_type=MESH
        )
    pl.semaphore_wait(barrier, len(chip_bits) + 1 + 3)

    class Gather:
        def __init__(self, index, land, slot):
            self.index, self.land, self.slot = index, land, slot
            self.orders = [
                chip_bits + [core_bit],
                chip_bits[1:] + chip_bits[:1] + [core_bit],
            ]

        def copy(self, h, mask, bit):
            block = self.land.at[moved(mask), pl.ds(h * half, half)]
            return pltpu.make_async_remote_copy(
                src_ref=block,
                dst_ref=block,
                send_sem=send_sem.at[self.index, h, mask ^ bit],
                recv_sem=recv_sem.at[self.index, h, mask ^ bit],
                device_id=(layer, moved(bit)),
                device_id_type=MESH,
            )

        def later(self, h, mask):
            order_h = self.orders[h]
            last = max([i for i, b in enumerate(order_h) if mask & b], default=-1)
            return order_h[last + 1:]

        def start(self):
            for k in range(len(self.orders[0])):
                for h in range(2):
                    self.copy(h, 0, self.orders[h][k]).start()

        def convert(self, h, mask):
            place = moved(mask)
            block = self.land[place, h * half:(h + 1) * half]
            high = block.astype(jnp.bfloat16)
            where = pl.ds(pl.multiple_of(place * rows + h * half, half), half)
            whi[self.slot, where] = high
            wlo[self.slot, where] = (block - high.astype(jnp.float32)).astype(jnp.bfloat16)

        def masks(self):
            found = []
            for k in range(len(self.orders[0])):
                for low in range(1 << k):
                    for h in range(2):
                        mask = self.orders[h][k]
                        for i in range(k):
                            if low >> i & 1:
                                mask |= self.orders[h][i]
                        found.append((h, mask))
            return found

        def arrive(self, h, mask):
            block = self.land.at[moved(mask), pl.ds(h * half, half)]
            pltpu.make_async_remote_copy(
                src_ref=block,
                dst_ref=block,
                send_sem=send_sem.at[self.index, h, mask],
                recv_sem=recv_sem.at[self.index, h, mask],
                device_id=(layer, moved(core_bit)),
                device_id_type=MESH,
            ).wait_recv()
            for bit in self.later(h, mask):
                self.copy(h, mask, bit).start()

        def relay(self):
            for h, mask in self.masks():
                if len(self.later(h, mask)) > 1:
                    self.arrive(h, mask)

        def finish(self):
            for h in range(2):
                self.convert(h, 0)
            for h, mask in self.masks():
                if len(self.later(h, mask)) <= 1:
                    self.arrive(h, mask)
                self.convert(h, mask)

        def sent(self):
            for h, mask in self.masks():
                order_h = self.orders[h]
                bit = [b for b in order_h if mask & b][-1]
                self.copy(h, mask ^ bit, bit).wait_send()

    def zcopy(src, dst, send, recv, to):
        return pltpu.make_async_remote_copy(
            src_ref=src,
            dst_ref=dst,
            send_sem=zsend.at[send],
            recv_sem=zrecv.at[recv],
            device_id=(to, me),
            device_id_type=MESH,
        )

    def put(m, value):
        high = value.astype(jnp.bfloat16)
        lhs[0:m] = high
        lhs[m:2 * m] = (value - high.astype(jnp.float32)).astype(jnp.bfloat16)

    def multiply(m, slot, dst):
        @pl.loop(0, order // TILE)
        def _(t):
            cols = pl.ds(pl.multiple_of(t * TILE, TILE), TILE)
            large = jnp.dot(lhs[0:2 * m], whi[slot, :, cols], preferred_element_type=jnp.float32)
            small = jnp.dot(lhs[0:m], wlo[slot, :, cols], preferred_element_type=jnp.float32)
            dst[0:m, cols] = large[0:m] + large[m:2 * m] + small

    g_f = Gather(0, land_f, 0)
    g_ra = Gather(1, land_ra, 1)
    g_rb = Gather(2, land_rb, 2)
    g_ta = Gather(3, land_ta, 0)
    g_h1 = Gather(4, land_h1, 1)
    g_h2 = Gather(5, land_h2, 2)
    g_l = Gather(6, land_l, 0)

    land_f[me] = refl_ref[...]
    g_f.start()
    decays = decay_ref[...]
    now[0:rows] = own_decay_ref[...] * refl_ref[...]
    row_ids = me * rows + lax.broadcasted_iota(jnp.int32, (rows, order), 0)
    col_ids = lax.broadcasted_iota(jnp.int32, (rows, order), 1)
    acc[0:rows] = jnp.where(row_ids == col_ids, 1.0, 0.0).astype(jnp.float32)
    acc[rows:2 * rows] = now[0:rows]
    g_f.relay()
    g_f.finish()

    @pl.loop(0, TERMS - 1)
    def _(_k):
        put(rows, now[0:rows] * decay_ref[...])
        multiply(rows, 0, now)
        acc[0:rows] += now[0:rows]
        put(rows, now[0:rows] * decay_ref[...])
        multiply(rows, 0, now)
        acc[rows:2 * rows] += now[0:rows]

    put(2 * rows, acc[...])
    multiply(2 * rows, 0, mid)
    land_ra[me] = acc[rows:2 * rows] * decays - mid[0:rows]
    land_ta[me] = acc[0:rows] * decays - mid[rows:2 * rows]

    partner = layer + 1 - 2 * (layer % 2)
    r_across = zcopy(land_ra.at[me], land_rb.at[me], 0, 0, partner)
    t_across = zcopy(land_ta.at[me], t_other, 1, 1, partner)
    r_across.start()
    g_ra.start()
    g_ra.relay()
    r_across.wait_recv()
    t_across.start()
    g_rb.start()
    g_ra.finish()
    g_rb.relay()
    g_ta.start()
    g_rb.finish()
    put(rows, land_ta[me])
    multiply(rows, 2, now)
    t_across.wait_recv()
    now[rows:2 * rows] = t_other[...]
    acc[...] = now[...]

    def first_chain(_k):
        put(2 * rows, now[...])
        multiply(2 * rows, 1, mid)
        put(2 * rows, mid[...])
        multiply(2 * rows, 2, now)
        acc[...] += now[...]

    pl.loop(0, 2)(first_chain)
    g_ta.relay()
    pl.loop(2, TERMS - 1)(first_chain)
    g_ta.finish()
    put(2 * rows, acc[...])
    multiply(2 * rows, 0, mid)
    out1[...] = land_ra[me] + mid[0:rows]
    out2[...] = mid[rows:2 * rows]

    beside = layer * 3 - 3
    other = 3 - layer
    to_last = 2 - layer // 3
    h1_near = zcopy(out1, land_h1.at[me], 2, 2, beside)
    h2_across = zcopy(out1, land_h2.at[me], 3, 3, other)
    s_near = zcopy(out2, start1, 4, 4, beside)
    l_far = zcopy(out2, land_l.at[me], 5, 5, to_last)
    h2_on = zcopy(land_h2.at[me], land_h2.at[me], 6, 3, beside)
    h1_in = zcopy(land_h1.at[me], land_h1.at[me], 2, 2, other)
    h2_in = zcopy(land_h2.at[me], land_h2.at[me], 3, 3, other)
    s_in = zcopy(start1, start1, 4, 4, other)
    l_in = zcopy(land_l.at[me], land_l.at[me], 5, 5, other)

    @pl.when(inner)
    def _():
        h1_near.start()
        h2_across.start()
        land_h1[me] = out1[...]
        now[0:rows] = out2[...]

    @pl.when(outer)
    def _():
        land_l[me] = out2[...]
        h1_in.wait_recv()
        l_far.start()

    g_h1.start()
    g_h1.relay()
    h2_in.wait_recv()

    @pl.when(inner)
    def _():
        h2_on.start()
        s_near.start()

    g_h2.start()
    g_h1.finish()
    g_h2.relay()

    @pl.when(inner)
    def _():
        l_in.wait_recv()

    g_l.start()
    g_h2.finish()

    @pl.when(outer)
    def _():
        s_in.wait_recv()
        now[0:rows] = start1[...]

    acc[0:rows] = now[0:rows]

    def second_chain(_k):
        put(rows, now[0:rows])
        multiply(rows, 2, mid)
        put(rows, mid[0:rows])
        multiply(rows, 1, now)
        acc[0:rows] += now[0:rows]

    pl.loop(0, 3)(second_chain)
    g_l.relay()
    pl.loop(3, TERMS - 1)(second_chain)

    @pl.when(outer)
    def _():
        put(rows, acc[0:rows])
        multiply(rows, 2, acc)

    g_l.finish()
    put(rows, acc[0:rows])
    multiply(rows, 0, mid)

    @pl.when(inner)
    def _():
        out_ref[0] = mid[0:rows]

    @pl.when(outer)
    def _():
        out_ref[0] = mid[0:rows] + out1[...]

    for gather in (g_f, g_ra, g_rb, g_ta, g_h1, g_h2, g_l):
        gather.sent()
    r_across.wait_send()
    t_across.wait_send()

    @pl.when(inner)
    def _():
        for copy in (h1_near, h2_across, s_near, h2_on):
            copy.wait_send()

    @pl.when(outer)
    def _():
        l_far.wait_send()


def local(n, reflections, wave_decay, thickness, material):
    rows, order = reflections.shape[1:]
    me = lax.axis_index("panel")
    chosen = material[0]
    refl_rows = lax.dynamic_index_in_dim(reflections, chosen, 0, keepdims=False)
    decays = jnp.exp(
        -lax.dynamic_index_in_dim(wave_decay, chosen, 0, keepdims=False) * thickness[0]
    )
    own_decays = lax.dynamic_slice_in_dim(decays, me * rows, rows)
    whole = pltpu.VMEM((n, rows, order), jnp.float32)
    pair = pltpu.VMEM((2 * rows, order), jnp.float32)
    one = pltpu.VMEM((rows, order), jnp.float32)
    factors = pltpu.VMEM((3, order, order), jnp.bfloat16)
    return pl.pallas_call(
        functools.partial(kernel, n, rows, order),
        out_shape=jax.ShapeDtypeStruct((1, rows, order), jnp.float32),
        in_specs=[pl.BlockSpec(memory_space=pltpu.VMEM)] * 3,
        out_specs=pl.BlockSpec(memory_space=pltpu.VMEM),
        scratch_shapes=[whole] * 7 + [factors] * 2
        + [pltpu.VMEM((4 * rows, order), jnp.bfloat16)]
        + [pair] * 3 + [one] * 4
        + [pltpu.SemaphoreType.DMA((7, 2, n))] * 2
        + [pltpu.SemaphoreType.DMA((7,))] * 2,
        compiler_params=pltpu.CompilerParams(
            collective_id=0, has_side_effects=True, vmem_limit_bytes=58 * 2**20
        ),
    )(refl_rows, decays[None, :], own_decays[:, None])


def solution(mesh):
    placed = (P(None, "panel", None), P(), P("layer"), P("layer"))
    return jax.shard_map(
        functools.partial(local, mesh.shape["panel"]),
        mesh=mesh, in_specs=placed, out_specs=P("layer", "panel", None), check_vma=False,
    )
```

```python
import functools

import jax
import jax.numpy as jnp
from jax import lax
from jax.experimental import pallas as pl
from jax.experimental.pallas import tpu as pltpu
from jax.sharding import PartitionSpec as P

TERMS = 6
TILE = 256
MESH = pl.DeviceIdType.MESH


def kernel(
    n, rows, order,
    refl_ref, decay_ref, own_decay_ref, out_ref,
    land_f, land_ra, land_rb, land_ta, land_h1, land_h2, land_l,
    whi, wlo, lhs, now, mid, acc, t_other, start1, out1, out2,
    send_sem, recv_sem, zsend, zrecv,
):
    layer = lax.axis_index("layer")
    me = lax.axis_index("panel")
    half = rows // 2
    core_bit = 1
    chip_bits = [1 << i for i in range(1, n.bit_length() - 1)]
    inner = (layer == 1) | (layer == 2)
    outer = (layer == 0) | (layer == 3)

    def moved(mask):
        place = me
        bit = 1
        while bit < n:
            if mask & bit:
                place = place + bit * (1 - 2 * (me // bit % 2))
            bit *= 2
        return place

    barrier = pltpu.get_barrier_semaphore()
    for bit in chip_bits + [core_bit]:
        pl.semaphore_signal(barrier, inc=1, device_id=(layer, moved(bit)), device_id_type=MESH)
    for step in range(1, 4):
        pl.semaphore_signal(
            barrier, inc=1, device_id=((layer + step) % 4, me), device_id_type=MESH
        )
    pl.semaphore_wait(barrier, len(chip_bits) + 1 + 3)

    class Gather:
        def __init__(self, index, land, slot):
            self.index, self.land, self.slot = index, land, slot
            self.orders = [
                chip_bits + [core_bit],
                chip_bits[1:] + chip_bits[:1] + [core_bit],
            ]

        def copy(self, h, mask, bit):
            block = self.land.at[moved(mask), pl.ds(h * half, half)]
            return pltpu.make_async_remote_copy(
                src_ref=block,
                dst_ref=block,
                send_sem=send_sem.at[self.index, h, mask ^ bit],
                recv_sem=recv_sem.at[self.index, h, mask ^ bit],
                device_id=(layer, moved(bit)),
                device_id_type=MESH,
            )

        def later(self, h, mask):
            order_h = self.orders[h]
            last = max([i for i, b in enumerate(order_h) if mask & b], default=-1)
            return order_h[last + 1:]

        def start(self, halves=(0, 1)):
            for k in range(len(self.orders[0])):
                for h in halves:
                    self.copy(h, 0, self.orders[h][k]).start()

        def convert(self, h, mask):
            place = moved(mask)
            block = self.land[place, h * half:(h + 1) * half]
            high = block.astype(jnp.bfloat16)
            where = pl.ds(pl.multiple_of(place * rows + h * half, half), half)
            whi[self.slot, where] = high
            wlo[self.slot, where] = (block - high.astype(jnp.float32)).astype(jnp.bfloat16)

        def masks(self):
            found = []
            for k in range(len(self.orders[0])):
                for low in range(1 << k):
                    for h in range(2):
                        mask = self.orders[h][k]
                        for i in range(k):
                            if low >> i & 1:
                                mask |= self.orders[h][i]
                        found.append((h, mask))
            return found

        def arrive(self, h, mask):
            block = self.land.at[moved(mask), pl.ds(h * half, half)]
            pltpu.make_async_remote_copy(
                src_ref=block,
                dst_ref=block,
                send_sem=send_sem.at[self.index, h, mask],
                recv_sem=recv_sem.at[self.index, h, mask],
                device_id=(layer, moved(core_bit)),
                device_id_type=MESH,
            ).wait_recv()
            for bit in self.later(h, mask):
                self.copy(h, mask, bit).start()

        def relay(self):
            for h, mask in self.masks():
                if len(self.later(h, mask)) > 1:
                    self.arrive(h, mask)

        def finish(self):
            for h in range(2):
                self.convert(h, 0)
            for h, mask in self.masks():
                if len(self.later(h, mask)) <= 1:
                    self.arrive(h, mask)
                self.convert(h, mask)

        def sent(self):
            for h, mask in self.masks():
                order_h = self.orders[h]
                bit = [b for b in order_h if mask & b][-1]
                self.copy(h, mask ^ bit, bit).wait_send()

    def zcopy(src, dst, send, recv, to):
        return pltpu.make_async_remote_copy(
            src_ref=src,
            dst_ref=dst,
            send_sem=zsend.at[send],
            recv_sem=zrecv.at[recv],
            device_id=(to, me),
            device_id_type=MESH,
        )

    def split(buffer, m, cols, value):
        high = value.astype(jnp.bfloat16)
        lhs[buffer, 0:m, cols] = high
        lhs[buffer, m:2 * m, cols] = (value - high.astype(jnp.float32)).astype(jnp.bfloat16)

    def put(buffer, m, value):
        split(buffer, m, slice(None), value)

    def multiply(m, slot, buffer, emit):
        for t in range(order // TILE):
            cols = slice(t * TILE, (t + 1) * TILE)
            large = jnp.dot(
                lhs[buffer, 0:2 * m], whi[slot, :, cols], preferred_element_type=jnp.float32
            )
            small = jnp.dot(
                lhs[buffer, 0:m], wlo[slot, :, cols], preferred_element_type=jnp.float32
            )
            emit(cols, large[0:m] + large[m:2 * m] + small)

    def store(dst, m):
        def emit(cols, value):
            dst[0:m, cols] = value

        return emit

    def powers(m, first, second, relay_at, relay):
        put(0, m, acc[0:m])

        def after_second(cols, value):
            acc[0:m, cols] += value
            split(0, m, cols, value)

        @pl.loop(0, TERMS - 1)
        def _(k):
            multiply(m, first, 0, functools.partial(split, 1, m))
            multiply(m, second, 1, after_second)
            pl.when(k == relay_at)(relay)

    g_f = Gather(0, land_f, 0)
    g_ra = Gather(1, land_ra, 1)
    g_rb = Gather(2, land_rb, 2)
    g_ta = Gather(3, land_ta, 0)
    g_h1 = Gather(4, land_h1, 1)
    g_h2 = Gather(5, land_h2, 2)
    g_l = Gather(6, land_l, 0)

    land_f[me] = refl_ref[...]
    g_f.start()
    decays = decay_ref[...]
    now[0:rows] = own_decay_ref[...] * refl_ref[...]
    row_ids = me * rows + lax.broadcasted_iota(jnp.int32, (rows, order), 0)
    col_ids = lax.broadcasted_iota(jnp.int32, (rows, order), 1)
    acc[0:rows] = jnp.where(row_ids == col_ids, 1.0, 0.0).astype(jnp.float32)
    acc[rows:2 * rows] = now[0:rows]
    g_f.relay()
    g_f.finish()

    put(0, rows, now[0:rows] * decays)

    def after_layer(at, buffer):
        def emit(cols, value):
            acc[at:at + rows, cols] += value
            split(buffer, rows, cols, value * decay_ref[:, cols])

        return emit

    @pl.loop(0, TERMS - 1)
    def _(_k):
        multiply(rows, 0, 0, after_layer(0, 1))
        multiply(rows, 0, 1, after_layer(rows, 0))

    put(0, 2 * rows, acc[...])
    multiply(2 * rows, 0, 0, store(mid, 2 * rows))
    land_ra[me] = acc[rows:2 * rows] * decays - mid[0:rows]
    land_ta[me] = acc[0:rows] * decays - mid[rows:2 * rows]

    partner = layer + 1 - 2 * (layer % 2)
    r_across = zcopy(land_ra.at[me], land_rb.at[me], 0, 0, partner)
    t_across = zcopy(land_ta.at[me], t_other, 1, 1, partner)
    r_across.start()
    g_ra.start()
    g_ra.relay()
    r_across.wait_recv()
    t_across.start()
    g_rb.start()
    g_ra.finish()
    g_rb.relay()
    g_ta.start()
    g_rb.finish()
    put(0, rows, land_ta[me])
    multiply(rows, 2, 0, store(acc, rows))
    t_across.wait_recv()
    acc[rows:2 * rows] = t_other[...]
    powers(2 * rows, 1, 2, 1, g_ta.relay)
    g_ta.finish()
    put(0, 2 * rows, acc[...])
    multiply(2 * rows, 0, 0, store(mid, 2 * rows))
    out1[...] = land_ra[me] + mid[0:rows]
    out2[...] = mid[rows:2 * rows]

    beside = layer * 3 - 3
    other = 3 - layer
    to_last = 2 - layer // 3
    parts = [pl.ds(0, half), pl.ds(half, half)]
    h1_near = [
        zcopy(out1.at[part], land_h1.at[me, part], sem, sem, beside)
        for part, sem in zip(parts, (2, 7))
    ]
    h2_across = zcopy(out1, land_h2.at[me], 3, 3, other)
    s_near = zcopy(out2, start1, 4, 4, beside)
    l_far = zcopy(out2, land_l.at[me], 5, 5, to_last)
    h2_on = zcopy(land_h2.at[me], land_h2.at[me], 6, 3, beside)
    h1_in = [
        zcopy(land_h1.at[me, part], land_h1.at[me, part], sem, sem, other)
        for part, sem in zip(parts, (2, 7))
    ]
    h2_in = zcopy(land_h2.at[me], land_h2.at[me], 3, 3, other)
    s_in = zcopy(start1, start1, 4, 4, other)
    l_in = zcopy(land_l.at[me], land_l.at[me], 5, 5, other)

    @pl.when(inner)
    def _():
        for copy in h1_near:
            copy.start()
        h2_across.start()
        land_h1[me] = out1[...]
        acc[0:rows] = out2[...]

    @pl.when(outer)
    def _():
        land_l[me] = out2[...]
        h1_in[0].wait_recv()

    g_h1.start((0,))

    @pl.when(outer)
    def _():
        h1_in[1].wait_recv()
        l_far.start()

    g_h1.start((1,))
    g_h1.relay()
    h2_in.wait_recv()

    @pl.when(inner)
    def _():
        h2_on.start()
        s_near.start()

    g_h2.start()
    g_h1.finish()
    g_h2.relay()

    @pl.when(inner)
    def _():
        l_in.wait_recv()

    g_l.start()
    g_h2.finish()

    @pl.when(outer)
    def _():
        s_in.wait_recv()
        acc[0:rows] = start1[...]

    powers(rows, 2, 1, 2, g_l.relay)

    @pl.when(outer)
    def _():
        put(0, rows, acc[0:rows])
        multiply(rows, 2, 0, store(acc, rows))

    g_l.finish()
    put(0, rows, acc[0:rows])
    multiply(rows, 0, 0, store(mid, rows))

    @pl.when(inner)
    def _():
        out_ref[0] = mid[0:rows]

    @pl.when(outer)
    def _():
        out_ref[0] = mid[0:rows] + out1[...]

    for gather in (g_f, g_ra, g_rb, g_ta, g_h1, g_h2, g_l):
        gather.sent()
    r_across.wait_send()
    t_across.wait_send()

    @pl.when(inner)
    def _():
        for copy in (*h1_near, h2_across, s_near, h2_on):
            copy.wait_send()

    @pl.when(outer)
    def _():
        l_far.wait_send()


def local(n, reflections, wave_decay, thickness, material):
    rows, order = reflections.shape[1:]
    me = lax.axis_index("panel")
    chosen = material[0]
    refl_rows = lax.dynamic_index_in_dim(reflections, chosen, 0, keepdims=False)
    decays = jnp.exp(
        -lax.dynamic_index_in_dim(wave_decay, chosen, 0, keepdims=False) * thickness[0]
    )
    own_decays = lax.dynamic_slice_in_dim(decays, me * rows, rows)
    whole = pltpu.VMEM((n, rows, order), jnp.float32)
    pair = pltpu.VMEM((2 * rows, order), jnp.float32)
    one = pltpu.VMEM((rows, order), jnp.float32)
    factors = pltpu.VMEM((3, order, order), jnp.bfloat16)
    return pl.pallas_call(
        functools.partial(kernel, n, rows, order),
        out_shape=jax.ShapeDtypeStruct((1, rows, order), jnp.float32),
        in_specs=[pl.BlockSpec(memory_space=pltpu.VMEM)] * 3,
        out_specs=pl.BlockSpec(memory_space=pltpu.VMEM),
        scratch_shapes=[whole] * 7 + [factors] * 2
        + [pltpu.VMEM((2, 4 * rows, order), jnp.bfloat16)]
        + [pair] * 3 + [one] * 4
        + [pltpu.SemaphoreType.DMA((7, 2, n))] * 2
        + [pltpu.SemaphoreType.DMA((8,))] * 2,
        compiler_params=pltpu.CompilerParams(
            collective_id=0, has_side_effects=True, vmem_limit_bytes=58 * 2**20
        ),
    )(refl_rows, decays[None, :], own_decays[:, None])


def solution(mesh):
    placed = (P(None, "panel", None), P(), P("layer"), P("layer"))
    return jax.shard_map(
        functools.partial(local, mesh.shape["panel"]),
        mesh=mesh, in_specs=placed, out_specs=P("layer", "panel", None), check_vma=False,
    )
```
